1024 devices in a mesh: dp: 64 (over y, x, core), expert: 16 (over z).
Axes of the slice: x: 4, y: 8, z: 16, core: 2. Of those that a mesh axis runs over, the one named last changes fastest.
Arguments:
- grad_out: bfloat16 [1024, 3200], P('expert', 'dp'), may hold values from -6 to 6
- expert_index: int32 [1024], P('expert'), may hold values from 0 to 15, as said below
- slot_index: int32 [1024], P('expert'), may hold values from 0 to 4, as said below
- capacity: int32 [16], replicated, may hold values from 2 to 5, as said below
- router_share: float32 [1024], P('expert'), may hold values from 0.2 to 1
- routed_gate: bfloat16 [16, 80, 9216], P('expert', None, 'dp'), may hold values from -6 to 6
- routed_up: bfloat16 [16, 80, 9216], P('expert', None, 'dp'), may hold values from -6 to 6
- gate_weight: bfloat16 [16, 9216, 3200], P('expert', 'dp'), may hold values from -0.3125 to 0.3125
- up_weight: bfloat16 [16, 9216, 3200], P('expert', 'dp'), may hold values from -0.3125 to 0.3125
- down_weight: bfloat16 [16, 9216, 3200], P('expert', 'dp'), may hold values from -0.0625 to 0.0625
- shared_gate: bfloat16 [1024, 9216], P('expert', 'dp'), may hold values from -6 to 6
- shared_up: bfloat16 [1024, 9216], P('expert', 'dp'), may hold values from -6 to 6
- gate_common: bfloat16 [9216, 3200], P('dp'), may hold values from -0.3125 to 0.3125
- up_common: bfloat16 [9216, 3200], P('dp'), may hold values from -0.3125 to 0.3125
- down_common: bfloat16 [9216, 3200], P('dp'), may hold values from -0.0625 to 0.0625
Outputs:
- input_grad: bfloat16 [1024, 3200], P('expert', 'dp')
The draws below stay inside these ranges and needn't reach their ends.
Inputs may be any that keep to these rules, and one draw needn't show every extreme that they name: `expert_index`: in each block of 64 tokens no expert is named more than 5 times, and one expert, the same in every block, is named exactly 5 times in every block. `slot_index`: the rank of the token among the tokens of its block that name the same expert, counted in token order from 0. The expert that is named 5 times in every block has capacity 5.
All inputs are finite; a program needn't handle non-finite values.
Results may differ from the reference program's by a relative error of at most 0.0052.
Values may be sent and summed in bfloat16 or wider, within the bound.
A program may use at most 32 MiB of HBM per device.

```python
import jax
import jax.numpy as jnp
from jax import lax

D = 3200
FR = 9216
FS = 9216
TOK_BLK = 64
EXPERTS = 16
CAP = 5
ROWS = 80
TOKENS = 1024
N_EXPERT = 16


def shuffle(sub_key):
    return jax.random.permutation(sub_key, TOK_BLK)


def routing_tables(key):
    level_key, score_key, order_key, full_key = jax.random.split(key, 4)
    full_expert = jax.random.randint(full_key, (), 0, EXPERTS)
    levels = jax.random.randint(level_key, (EXPERTS,), 0, 3)
    pair_ids = jnp.arange(EXPERTS * CAP, dtype=jnp.int32)
    pair_expert = pair_ids // CAP
    noise_draw = jax.random.randint(score_key, (N_EXPERT, EXPERTS * CAP), 0, 65536)
    favored = (pair_expert == full_expert).astype(jnp.int32)
    scores = (noise_draw + levels[pair_expert][None, :] * 65536 + favored[None, :] * 262144) * 2048 + pair_ids[None, :]
    top_scores, chosen = lax.top_k(scores, TOK_BLK)
    chosen_expert = chosen // CAP
    orders = jax.vmap(shuffle)(jax.random.split(order_key, N_EXPERT))
    token_expert = jnp.take_along_axis(chosen_expert, orders, axis=1).astype(jnp.int32)
    onehot = (token_expert[:, :, None] == jnp.arange(EXPERTS, dtype=jnp.int32)[None, None, :]).astype(jnp.int32)
    before = jnp.cumsum(onehot, axis=1) - onehot
    slot_ranks = jnp.sum(before * onehot, axis=2)
    return (token_expert.reshape(TOKENS), slot_ranks.reshape(TOKENS).astype(jnp.int32), full_expert)


def draw_expert_index(key, part):
    return routing_tables(key)[0]


def draw_slot_index(key, part):
    return routing_tables(key)[1]


def draw_capacity(key, part):
    full_expert = routing_tables(key)[2]
    key = jax.random.fold_in(key, 7)
    lowest = CAP // 2
    values = jax.random.randint(key, (EXPERTS,), lowest, CAP + 1)
    expert_ids = jnp.arange(EXPERTS, dtype=jnp.int32)
    values = jnp.where(expert_ids == (full_expert + 1) % EXPERTS, lowest, values)
    return jnp.where(expert_ids == full_expert, CAP, values).astype(jnp.int32)


def spiked(array, rng, source, target, shards_of, factor):
    owner, partner = [(jnp.arange(array.shape[dim]) // (array.shape[dim] // shards_of)).reshape([-1 if axis == dim else 1 for axis in range(array.ndim)]) for dim in (source, target)]
    chosen = jax.random.permutation(rng, shards_of)[partner]
    strong = (owner == chosen) | (owner == (partner + shards_of // 2) % shards_of)
    return jnp.where(strong, factor * array, array)


def steps_of(stream_key, dims, cuts, least, largest):
    factor_of = 1.0
    for position, parts in cuts:
        steps = jax.random.uniform(jax.random.fold_in(jax.random.fold_in(stream_key, 6), position), (parts,), jnp.float32, least / len(cuts), largest / len(cuts))
        factor_of = factor_of * jnp.repeat(jnp.exp(steps), dims[position] // parts).reshape((-1,) + (1,) * (len(dims) - 1 - position))
    return factor_of


def centred(rng, dims, scale, bound, cuts=(), kind=jnp.bfloat16):
    array = scale * jax.random.normal(rng, dims, jnp.float32)
    if cuts:
        array = array * steps_of(rng, dims, cuts, -0.22, 0.18)
    return jnp.clip(array, -bound, bound).astype(kind)


def heavy_noise(rng, extent, spread, most, cuts, heavy, kind=jnp.bfloat16):
    result = spread * jax.random.normal(rng, extent, jnp.float32)
    if cuts:
        result = result * steps_of(rng, extent, cuts, -0.22, 0.18)
    return jnp.clip(spiked(result, jax.random.fold_in(rng, 3), *heavy), -most, most).astype(kind)


def setup_inputs(seed: int = 0) -> dict:
    arg_keys = jax.random.split(jax.random.key(seed), 16)
    grad_out = centred(arg_keys[0], (TOKENS, D), 1.0, 6.0, ((0, 16), (1, 64)))
    expert_index = draw_expert_index(jax.random.fold_in(arg_keys[15], 71), 0)
    slot_index = draw_slot_index(jax.random.fold_in(arg_keys[15], 71), 0)
    capacity = draw_capacity(jax.random.fold_in(arg_keys[15], 71), 0)
    router_share = jnp.clip(0.2 + 0.8 * jax.random.uniform(arg_keys[4], (TOKENS,), jnp.float32) ** steps_of(arg_keys[4], (TOKENS,), ((0, 16),), -0.2, 0.2), 0.2, 1.0)
    routed_gate = centred(arg_keys[5], (EXPERTS, ROWS, FR), 1.0, 6.0, ((0, 16), (2, 64)))
    routed_up = centred(arg_keys[6], (EXPERTS, ROWS, FR), 1.0, 6.0, ((0, 16), (2, 64)))
    gate_weight = heavy_noise(arg_keys[7], (EXPERTS, FR, D), D ** -0.5, 0.3125, ((0, 16), (1, 64)), (1, 2, 64, 4.0))
    up_weight = heavy_noise(arg_keys[8], (EXPERTS, FR, D), D ** -0.5, 0.3125, ((0, 16), (1, 64)), (1, 2, 64, 4.0))
    down_weight = centred(arg_keys[9], (EXPERTS, FR, D), FR ** -0.5, 0.0625, ((0, 16), (1, 64)))
    shared_gate = centred(arg_keys[10], (TOKENS, FS), 1.0, 6.0, ((0, 16), (1, 64)))
    shared_up = centred(arg_keys[11], (TOKENS, FS), 1.0, 6.0, ((0, 16), (1, 64)))
    gate_common = heavy_noise(arg_keys[12], (FS, D), D ** -0.5, 0.3125, ((0, 64),), (0, 1, 64, 4.0))
    up_common = heavy_noise(arg_keys[13], (FS, D), D ** -0.5, 0.3125, ((0, 64),), (0, 1, 64, 4.0))
    down_common = centred(arg_keys[14], (FS, D), FS ** -0.5, 0.0625, ((0, 64),))
    return {"grad_out": grad_out, "expert_index": expert_index, "slot_index": slot_index, "capacity": capacity, "router_share": router_share, "routed_gate": routed_gate, "routed_up": routed_up, "gate_weight": gate_weight, "up_weight": up_weight, "down_weight": down_weight, "shared_gate": shared_gate, "shared_up": shared_up, "gate_common": gate_common, "up_common": up_common, "down_common": down_common}


def silu_grads(grad_hidden, gate_pre, up_pre):
    gate_val = gate_pre.astype(jnp.float32)
    up_val = up_pre.astype(jnp.float32)
    sigmoid_gate = jax.nn.sigmoid(gate_val)
    grad_gate = grad_hidden * up_val * sigmoid_gate * (1.0 + gate_val * (1.0 - sigmoid_gate))
    grad_up = grad_hidden * gate_val * sigmoid_gate
    return grad_gate.astype(jnp.bfloat16), grad_up.astype(jnp.bfloat16)


def back_through(grad_rows, gate_pre, up_pre, gate_mat, up_mat, down_mat):
    grad_hidden = lax.dot_general(grad_rows, down_mat, (((1,), (1,)), ((), ())), preferred_element_type=jnp.float32)
    grad_gate, grad_up = silu_grads(grad_hidden, gate_pre, up_pre)
    first_term = jnp.dot(grad_gate, gate_mat, preferred_element_type=jnp.float32)
    second_term = jnp.dot(grad_up, up_mat, preferred_element_type=jnp.float32)
    return first_term + second_term


def reference(grad_out, expert_index, slot_index, capacity, router_share, routed_gate, routed_up, gate_weight, up_weight, down_weight, shared_gate, shared_up, gate_common, up_common, down_common):
    scaled = (router_share[:, None] * grad_out.astype(jnp.float32)).astype(jnp.bfloat16)
    onehot_cap = expert_index[:, None] == jnp.arange(EXPERTS, dtype=jnp.int32)[None, :]
    token_cap = jnp.sum(jnp.where(onehot_cap, capacity[None, :], 0), axis=1)
    keep_mask = slot_index < token_cap
    block_ids = jnp.arange(TOKENS, dtype=jnp.int32) // TOK_BLK
    target_row = block_ids * CAP + slot_index
    row_ids = jnp.arange(ROWS, dtype=jnp.int32)

    def one_expert(carry, inputs):
        expert_id, gate_pre, up_pre, gate_mat, up_mat, down_mat = inputs
        chosen = keep_mask & (expert_index == expert_id)
        placing = (row_ids[:, None] == target_row[None, :]) & chosen[None, :]
        grad_rows = jnp.dot(placing.astype(jnp.bfloat16), scaled, preferred_element_type=jnp.float32).astype(jnp.bfloat16)
        partial_rows = back_through(grad_rows, gate_pre, up_pre, gate_mat, up_mat, down_mat)
        back_rows = jnp.dot(placing.astype(jnp.float32).T, partial_rows, precision=lax.Precision.HIGHEST)
        return carry + back_rows, None

    routed_total, unused = lax.scan(one_expert, jnp.zeros((TOKENS, D), jnp.float32), (jnp.arange(EXPERTS, dtype=jnp.int32), routed_gate, routed_up, gate_weight, up_weight, down_weight))
    shared_part = back_through(grad_out, shared_gate, shared_up, gate_common, up_common, down_common)
    return (shared_part + routed_total).astype(jnp.bfloat16)
```

```python
import jax
import jax.numpy as jnp
from jax import lax
from jax.experimental import pallas as pl
from jax.experimental.pallas import tpu as pltpu
from jax.sharding import PartitionSpec as P

BF = jnp.bfloat16
F32 = jnp.float32
MESH = pl.DeviceIdType.MESH
NX, NY, NZ = 4, 8, 16
CHIPS = NX * NY
TOK = 64
CAP = 5
ROUTED = NZ * CAP
HID = 144
FEAT = 50
CHUNK = 2 * FEAT
LANES = 128
WIDTH = CHIPS * CHUNK
NEAR_FIRST = (1, 7, 2, 6, 3, 5, 4)
FAR_FIRST = (4, 3, 5, 2, 6, 1, 7, 0)
X_STEPS = (2, 1, 3)


def nt_dot(a, b):
    return lax.dot_general(a, b, (((1,), (1,)), ((), ())), preferred_element_type=F32)


def nn_dot(a, b):
    return lax.dot_general(a, b, (((1,), (0,)), ((), ())), preferred_element_type=F32)


def silu_grads(grad_hidden, gate_pre, up_pre):
    g = gate_pre.astype(F32)
    u = up_pre.astype(F32)
    s = 1.0 / (1.0 + jnp.exp(-g))
    dgate = grad_hidden * u * s * (1.0 + g * (1.0 - s))
    dup = grad_hidden * g * s
    return dgate.astype(BF), dup.astype(BF)


def kernel(
    x_hbm, eidx_hbm, slot_hbm, cap_hbm, share_hbm,
    rg_hbm, ru_hbm, gw_hbm, uw_hbm, dw_hbm,
    sg_hbm, su_hbm, gc_hbm, uc_hbm, dc_hbm,
    out_ref,
    x_mine, x_other, eidx, slot, cap, share,
    pre_rg, pre_ru, pre_sg, pre_su,
    raw, win, place,
    z_out, z_in, z2_out, z2_in, slots,
    rows_r, rows_s,
    part_out, part_in, four, own, sums, x_in, y_out, y_in,
    shared_sum, total,
    in_sem, pair_snd, pair_rcv, z_snd, z_rcv, z2_snd, z2_rcv,
    gy_snd, gy_rcv, gx_snd, gx_rcv, gs_snd, gs_rcv,
    p_snd, p_rcv, rx_snd, rx_rcv, ry_snd, ry_rcv,
):
    dp = lax.axis_index("dp")
    z = lax.axis_index("expert")
    core = lax.rem(dp, 2)
    chip = dp // 2
    x = lax.rem(chip, NX)
    y = chip // NX

    def at_y(k):
        yy = lax.rem(y + k, NY)
        return yy, ((yy * NX + x) * 2 + core, z)

    def at_x(k):
        xx = lax.rem(x + k, NX)
        return xx, ((y * NX + xx) * 2 + core, z)

    def at_z(k):
        zz = lax.rem(z + k, NZ)
        return zz, (dp, zz)

    sibling = (chip * 2 + 1 - core, z)

    def remote(src, dst, snd, rcv, dev):
        return pltpu.make_async_remote_copy(
            src_ref=src, dst_ref=dst, send_sem=snd, recv_sem=rcv, device_id=dev, device_id_type=MESH
        )

    barrier = pltpu.get_barrier_semaphore()
    pl.semaphore_signal(barrier, inc=1, device_id=sibling, device_id_type=MESH)
    for k in NEAR_FIRST:
        pl.semaphore_signal(barrier, inc=1, device_id=at_y(k)[1], device_id_type=MESH)
    for k in X_STEPS:
        pl.semaphore_signal(barrier, inc=1, device_id=at_x(k)[1], device_id_type=MESH)

    @pl.when(core == 0)
    def _():
        for k in range(1, NZ):
            pl.semaphore_signal(barrier, inc=1, device_id=at_z(k)[1], device_id_type=MESH)

    small = (
        (x_hbm, x_mine), (eidx_hbm, eidx), (slot_hbm, slot), (cap_hbm, cap), (share_hbm, share),
        (rg_hbm.at[0], pre_rg), (ru_hbm.at[0], pre_ru), (sg_hbm, pre_sg), (su_hbm, pre_su),
    )
    weights = (dc_hbm, gc_hbm, uc_hbm, dw_hbm.at[0], gw_hbm.at[0], uw_hbm.at[0])
    loads = [pltpu.make_async_copy(s, d, in_sem.at[i]) for i, (s, d) in enumerate(small)]
    for i, w in enumerate(weights):
        loads.append(pltpu.make_async_copy(w, raw.at[i, :, pl.ds(0, WIDTH)], in_sem.at[len(small) + i]))
    for c in loads:
        c.start()
    for i in range(6):
        raw[i, :, WIDTH:] = jnp.zeros((HID, LANES), BF)
    for c in loads[: len(small)]:
        c.wait()

    @pl.when(core == 0)
    def _():
        pl.semaphore_wait(barrier, 1 + NY - 1 + NX - 1 + NZ - 1)

    @pl.when(core == 1)
    def _():
        pl.semaphore_wait(barrier, 1 + NY - 1 + NX - 1)

    pair = remote(x_mine, x_other, pair_snd.at[0], pair_rcv.at[0], sibling)
    pair.start()

    def window(i):
        loads[len(small) + i].wait()
        for c in range(CHIPS):
            q, o = divmod(c * CHUNK, LANES)
            wide = raw[i, :, q * LANES : (q + 2) * LANES] if o else None
            piece = raw[i, :, q * LANES : (q + 1) * LANES] if o == 0 else wide[:, o : o + LANES]
            win[i, c // NX, :, (c % NX) * LANES : (c % NX + 1) * LANES] = piece

    lane = lax.broadcasted_iota(jnp.int32, (FEAT, LANES), 1)
    feat = lax.broadcasted_iota(jnp.int32, (FEAT, LANES), 0)
    put_mine = (lane == feat + FEAT * core).astype(BF)
    put_other = (lane == feat + FEAT * (1 - core)).astype(BF)

    def chip_rows():
        pair.wait()
        return (nn_dot(x_mine[...], put_mine) + nn_dot(x_other[...], put_other)).astype(BF)

    def send_y(rows):
        for k in NEAR_FIRST:
            remote(rows.at[y, x], rows.at[y, x], gy_snd.at[k], gy_rcv.at[k], at_y(k)[1]).start()

    def send_x(rows, k, yy):
        for j in X_STEPS:
            i = k * NX + j
            remote(rows.at[yy, x], rows.at[yy, x], gx_snd.at[i], gx_rcv.at[i], at_x(j)[1]).start()

    def relay_x(rows):
        send_x(rows, 0, y)
        for k in NEAR_FIRST:
            yy = lax.rem(y - k + NY, NY)
            remote(rows.at[yy, x], rows.at[yy, x], gy_snd.at[k], gy_rcv.at[k], at_y(k)[1]).wait_recv()
            send_x(rows, k, yy)

    def share_row(rows, k):
        yy = lax.rem(y - k + NY, NY)
        for j in X_STEPS:
            i = k * NX + j
            xx = lax.rem(x - j + NX, NX)
            remote(rows.at[yy, xx], rows.at[yy, xx], gx_snd.at[i], gx_rcv.at[i], at_x(j)[1]).wait_recv()
        remote(rows.at[yy], rows.at[yy], gs_snd.at[k], gs_rcv.at[k], sibling).start()
        return yy

    def take_row(rows, k):
        yy = lax.rem(y - k + NY, NY)
        remote(rows.at[yy], rows.at[yy], gs_snd.at[k], gs_rcv.at[k], sibling).wait_recv()
        return yy

    def hidden(rows, down, get_row):
        acc = None
        for k in (0,) + NEAR_FIRST:
            yy = get_row(rows, k)
            wide = jnp.concatenate([rows[yy, j] for j in range(NX)], axis=1)
            term = nt_dot(wide, win[down, yy])
            acc = term if acc is None else acc + term
        return acc

    def send_part(n, dg, du, gate, up):
        for k in FAR_FIRST:
            yy = lax.rem(y + k, NY)
            t = nn_dot(dg, win[gate, yy]) + nn_dot(du, win[up, yy])
            for j in range(NX):
                part_out[yy, j, 0:n] = t[:, j * LANES : (j + 1) * LANES].astype(BF)
            ref_out, ref_in = part_out.at[yy, :, pl.ds(0, n)], part_in.at[yy, :, pl.ds(0, n)]
            remote(ref_out, ref_in, p_snd.at[k], p_rcv.at[k], sibling).start()

    def own_part(n, dg, du, gate, up):
        for k in FAR_FIRST:
            yy = lax.rem(y + k, NY)
            t = nn_dot(dg, win[gate, yy]) + nn_dot(du, win[up, yy])
            ref_out, ref_in = part_out.at[yy, :, pl.ds(0, n)], part_in.at[yy, :, pl.ds(0, n)]
            remote(ref_out, ref_in, p_snd.at[k], p_rcv.at[k], sibling).wait_recv()
            for j in range(NX):
                s = t[:, j * LANES : (j + 1) * LANES] + part_in[yy, j, 0:n].astype(F32)
                four[j, 0:n] = s
                sums[yy, j, 0:n] = s.astype(BF)
            own[yy, 0:n] = four[x, 0:n]
            for j in X_STEPS:
                xx, dev = at_x(j)
                i = k * NX + j
                remote(
                    sums.at[yy, xx, pl.ds(0, n)], x_in.at[yy, j, pl.ds(0, n)],
                    rx_snd.at[i], rx_rcv.at[i], dev,
                ).start()

    def add_x(n, k):
        yy = lax.rem(y + k, NY)
        acc = own[yy, 0:n]
        for j in X_STEPS:
            i = k * NX + j
            remote(
                sums.at[yy, j, pl.ds(0, n)], x_in.at[yy, j, pl.ds(0, n)],
                rx_snd.at[i], rx_rcv.at[i], at_x(j)[1],
            ).wait_recv()
            acc += x_in[yy, j, 0:n].astype(F32)
        return acc

    def reduce(n):
        for k in FAR_FIRST[:-1]:
            y_out[k, 0:n] = add_x(n, k).astype(BF)
            remote(
                y_out.at[k, pl.ds(0, n)], y_in.at[k, pl.ds(0, n)], ry_snd.at[k], ry_rcv.at[k], at_y(k)[1]
            ).start()
        acc = add_x(n, 0)
        for k in NEAR_FIRST:
            remote(
                y_out.at[k, pl.ds(0, n)], y_in.at[k, pl.ds(0, n)], ry_snd.at[k], ry_rcv.at[k], at_y(k)[1]
            ).wait_recv()
            acc += y_in[k, 0:n].astype(F32)
        return acc

    def wait_sends(rows, n, other_n):
        for k in NEAR_FIRST:
            remote(rows.at[y, x], rows.at[y, x], gy_snd.at[k], gy_rcv.at[k], at_y(k)[1]).wait_send()
            remote(
                y_out.at[k, pl.ds(0, n)], y_in.at[k, pl.ds(0, n)], ry_snd.at[k], ry_rcv.at[k], at_y(k)[1]
            ).wait_send()
        for k in range(NY):
            remote(rows.at[y], rows.at[y], gs_snd.at[k], gs_rcv.at[k], sibling).wait_send()
            ref_out = part_out.at[k, :, pl.ds(0, other_n)]
            ref_in = part_in.at[k, :, pl.ds(0, other_n)]
            remote(ref_out, ref_in, p_snd.at[k], p_rcv.at[k], sibling).wait_send()
            for j in X_STEPS:
                i = k * NX + j
                remote(rows.at[y, x], rows.at[y, x], gx_snd.at[i], gx_rcv.at[i], at_x(j)[1]).wait_send()
                remote(
                    sums.at[k, j, pl.ds(0, n)], x_in.at[k, j, pl.ds(0, n)],
                    rx_snd.at[i], rx_rcv.at[i], at_x(j)[1],
                ).wait_send()

    answer = remote(shared_sum.at[0], shared_sum.at[1], pair_snd.at[1], pair_rcv.at[1], sibling)
    result = remote(total.at[0], total.at[1], pair_snd.at[2], pair_rcv.at[2], sibling)

    @pl.when(core == 0)
    def _():
        expert_row = eidx[...]
        token_cap = jnp.zeros((1, TOK), jnp.int32)
        for e in range(NZ):
            token_cap = jnp.where(expert_row == e, cap[:, e : e + 1], token_cap)
        target = expert_row * 8 + slot[...]
        row_ids = lax.broadcasted_iota(jnp.int32, (NZ * 8, TOK), 0)
        placing = ((row_ids == target) & (slot[...] < token_cap)).astype(F32)
        place[...] = placing.T
        eye = lax.broadcasted_iota(jnp.int32, (TOK, TOK), 0) == lax.broadcasted_iota(jnp.int32, (TOK, TOK), 1)
        share_col = jnp.sum(jnp.where(eye, share[...], 0.0), axis=1, keepdims=True)
        z2_out[...] = jnp.zeros_like(z2_out)
        scaled = (share_col * chip_rows().astype(F32)).astype(BF)
        z_out[...] = nn_dot(placing.astype(BF), scaled).reshape(NZ, 8, LANES)
        for k in range(1, NZ):
            zz, dev = at_z(k)
            remote(z_out.at[zz], z_in.at[z], z_snd.at[k], z_rcv.at[k], dev).start()
        z_in[z] = z_out[z]
        window(0)
        window(1)
        window(2)
        for k in range(1, NZ):
            zz = lax.rem(z - k + NZ, NZ)
            remote(z_out.at[zz], z_in.at[zz], z_snd.at[k], z_rcv.at[k], at_z(k)[1]).wait_recv()
        for b in range(NZ):
            slots[b * CAP : (b + 1) * CAP] = z_in[b, 0:CAP]
        rows_r[y, x] = slots[...].astype(BF)
        send_y(rows_r)
        window(3)
        relay_x(rows_r)
        dg, du = silu_grads(hidden(rows_s, 0, take_row), pre_sg[...], pre_su[...])
        send_part(TOK, dg, du, 1, 2)
        window(4)
        window(5)
        dg, du = silu_grads(hidden(rows_r, 3, share_row), pre_rg[...], pre_ru[...])
        own_part(ROUTED, dg, du, 4, 5)
        slots[...] = reduce(ROUTED)
        for b in range(NZ):
            z2_out[b, 0:CAP] = slots[b * CAP : (b + 1) * CAP]
        for k in range(1, NZ):
            zz, dev = at_z(k)
            remote(z2_out.at[zz], z2_in.at[z], z2_snd.at[k], z2_rcv.at[k], dev).start()
        z2_in[z] = z2_out[z]
        wait_sends(rows_r, ROUTED, TOK)
        for k in range(1, NZ):
            zz = lax.rem(z - k + NZ, NZ)
            remote(z2_out.at[zz], z2_in.at[zz], z2_snd.at[k], z2_rcv.at[k], at_z(k)[1]).wait_recv()
        back = z2_in[...].reshape(NZ * 8, LANES)
        picked = lax.dot_general(
            place[...], back, (((1,), (0,)), ((), ())),
            precision=lax.Precision.HIGHEST, preferred_element_type=F32,
        )
        answer.wait_recv()
        both = (shared_sum[1] + picked).astype(BF)
        total[0] = both
        result.start()
        out_ref[...] = both[:, 0:FEAT]
        for k in range(1, NZ):
            zz, dev = at_z(k)
            remote(z_out.at[zz], z_in.at[z], z_snd.at[k], z_rcv.at[k], dev).wait_send()
            remote(z2_out.at[zz], z2_in.at[z], z2_snd.at[k], z2_rcv.at[k], dev).wait_send()
        result.wait_send()

    @pl.when(core == 1)
    def _():
        rows_s[y, x] = chip_rows()
        send_y(rows_s)
        window(0)
        relay_x(rows_s)
        window(1)
        window(2)
        dg, du = silu_grads(hidden(rows_s, 0, share_row), pre_sg[...], pre_su[...])
        window(3)
        window(4)
        window(5)
        own_part(TOK, dg, du, 1, 2)
        dg, du = silu_grads(hidden(rows_r, 3, take_row), pre_rg[...], pre_ru[...])
        send_part(ROUTED, dg, du, 4, 5)
        shared_sum[0] = reduce(TOK)
        answer.start()
        wait_sends(rows_s, TOK, ROUTED)
        answer.wait_send()
        result.wait_recv()
        out_ref[...] = total[1][:, FEAT:CHUNK]


def body(
    grad_out, expert_index, slot_index, capacity, router_share,
    routed_gate, routed_up, gate_weight, up_weight, down_weight,
    shared_gate, shared_up, gate_common, up_common, down_common,
):
    dma = pltpu.SemaphoreType.DMA
    scratch = [
        pltpu.VMEM((TOK, FEAT), BF), pltpu.VMEM((TOK, FEAT), BF),
        pltpu.VMEM((1, TOK), jnp.int32), pltpu.VMEM((1, TOK), jnp.int32),
        pltpu.VMEM((1, NZ), jnp.int32), pltpu.VMEM((1, TOK), F32),
        pltpu.VMEM((ROUTED, HID), BF), pltpu.VMEM((ROUTED, HID), BF),
        pltpu.VMEM((TOK, HID), BF), pltpu.VMEM((TOK, HID), BF),
        pltpu.VMEM((6, HID, WIDTH + LANES), BF),
        pltpu.VMEM((6, NY, HID, NX * LANES), BF),
        pltpu.VMEM((TOK, NZ * 8), F32),
        pltpu.VMEM((NZ, 8, LANES), F32), pltpu.VMEM((NZ, 8, LANES), F32),
        pltpu.VMEM((NZ, 8, LANES), F32), pltpu.VMEM((NZ, 8, LANES), F32),
        pltpu.VMEM((ROUTED, LANES), F32),
        pltpu.VMEM((NY, NX, ROUTED, LANES), BF), pltpu.VMEM((NY, NX, TOK, LANES), BF),
        pltpu.VMEM((NY, NX, ROUTED, LANES), BF), pltpu.VMEM((NY, NX, ROUTED, LANES), BF),
        pltpu.VMEM((NX, ROUTED, LANES), F32), pltpu.VMEM((NY, ROUTED, LANES), F32),
        pltpu.VMEM((NY, NX, ROUTED, LANES), BF), pltpu.VMEM((NY, NX, ROUTED, LANES), BF),
        pltpu.VMEM((NY, ROUTED, LANES), BF), pltpu.VMEM((NY, ROUTED, LANES), BF),
        pltpu.VMEM((2, TOK, LANES), F32), pltpu.VMEM((2, TOK, LANES), BF),
        dma((15,)), dma((3,)), dma((3,)), dma((NZ,)), dma((NZ,)), dma((NZ,)), dma((NZ,)),
        dma((NY,)), dma((NY,)), dma((NY * NX,)), dma((NY * NX,)), dma((NY,)), dma((NY,)),
        dma((NY,)), dma((NY,)), dma((NY * NX,)), dma((NY * NX,)), dma((NY,)), dma((NY,)),
    ]
    return pl.pallas_call(
        kernel,
        out_shape=jax.ShapeDtypeStruct((TOK, FEAT), BF),
        in_specs=[pl.BlockSpec(memory_space=pl.ANY)] * 15,
        out_specs=pl.BlockSpec(memory_space=pltpu.VMEM),
        scratch_shapes=scratch,
        compiler_params=pltpu.CompilerParams(
            collective_id=0, has_side_effects=True, vmem_limit_bytes=56 * 1024 * 1024
        ),
    )(
        grad_out, expert_index.reshape(1, -1), slot_index.reshape(1, -1), capacity.reshape(1, -1),
        router_share.reshape(1, -1), routed_gate, routed_up, gate_weight, up_weight, down_weight,
        shared_gate, shared_up, gate_common, up_common, down_common,
    )


def solution(mesh):
    return jax.shard_map(
        body,
        mesh=mesh,
        in_specs=(
            P("expert", "dp"), P("expert"), P("expert"), P(), P("expert"),
            P("expert", None, "dp"), P("expert", None, "dp"),
            P("expert", "dp", None), P("expert", "dp", None), P("expert", "dp", None),
            P("expert", "dp"), P("expert", "dp"),
            P("dp", None), P("dp", None), P("dp", None),
        ),
        out_specs=P("expert", "dp"),
        check_vma=False,
    )
```

```python
import jax
import jax.numpy as jnp
from jax import lax
from jax.experimental import pallas as pl
from jax.experimental.pallas import tpu as pltpu
from jax.sharding import PartitionSpec as P

BF = jnp.bfloat16
F32 = jnp.float32
MESH = pl.DeviceIdType.MESH
NX, NY, NZ = 4, 8, 16
CHIPS = NX * NY
TOK = 64
CAP = 5
ROUTED = NZ * CAP
HID = 144
FEAT = 50
CHUNK = 2 * FEAT
LANES = 128
WIDTH = CHIPS * CHUNK
NEAR_FIRST = (1, 7, 2, 6, 3, 5, 4)
FAR_FIRST = (4, 3, 5, 2, 6, 1, 7, 0)
X_STEPS = (2, 1, 3)
Y_STEPS = (4, 3, 5, 2, 6, 1, 7)
Z_STEPS = (8, 7, 9, 6, 10, 5, 11, 4, 12, 3, 13, 2, 14, 1, 15)


def nt_dot(a, b):
    return lax.dot_general(a, b, (((1,), (1,)), ((), ())), preferred_element_type=F32)


def nn_dot(a, b):
    return lax.dot_general(a, b, (((1,), (0,)), ((), ())), preferred_element_type=F32)


def silu_factors(gate_pre, up_pre):
    g = gate_pre.astype(F32)
    u = up_pre.astype(F32)
    s = 1.0 / (1.0 + jnp.exp(-g))
    return u * s * (1.0 + g * (1.0 - s)), g * s


def kernel(
    x_hbm, eidx_hbm, slot_hbm, cap_hbm, share_hbm,
    rg_hbm, ru_hbm, gw_hbm, uw_hbm, dw_hbm,
    sg_hbm, su_hbm, gc_hbm, uc_hbm, dc_hbm,
    out_ref,
    x_mine, eidx, slot, cap, share,
    pre_r, pre_s, factor_r, factor_s, placed,
    raw, win, place,
    z_out, z_in, z2_out, z2_in, slots,
    rows_r, rows_s,
    four, own, sums, x_in, y_out, y_in,
    shared_sum,
    in_sem, pair_snd, pair_rcv, z_snd, z_rcv, z2_snd, z2_rcv,
    gy_snd, gy_rcv, gx_snd, gx_rcv, swap_snd, swap_rcv, rx_snd, rx_rcv, ry_snd, ry_rcv,
):
    dp = lax.axis_index("dp")
    z = lax.axis_index("expert")
    core = lax.rem(dp, 2)
    chip = dp // 2
    x = lax.rem(chip, NX)
    y = chip // NX

    def at_y(k):
        yy = lax.rem(y + k, NY)
        return yy, ((yy * NX + x) * 2 + core, z)

    def at_x(k):
        xx = lax.rem(x + k, NX)
        return xx, ((y * NX + xx) * 2 + core, z)

    def at_z(k, side):
        zz = lax.rem(z + k, NZ)
        return zz, (chip * 2 + side, zz)

    sibling = (chip * 2 + 1 - core, z)

    def remote(src, dst, snd, rcv, dev):
        return pltpu.make_async_remote_copy(
            src_ref=src, dst_ref=dst, send_sem=snd, recv_sem=rcv, device_id=dev, device_id_type=MESH
        )

    small = ((x_hbm, x_mine), (eidx_hbm, eidx), (slot_hbm, slot), (cap_hbm, cap), (share_hbm, share))
    loads = [pltpu.make_async_copy(s, d, in_sem.at[i]) for i, (s, d) in enumerate(small)]
    routed_in = (dw_hbm.at[0], gw_hbm.at[0], uw_hbm.at[0], rg_hbm.at[0], ru_hbm.at[0])
    shared_in = (dc_hbm, gc_hbm, uc_hbm, sg_hbm, su_hbm)

    def homes(half, pre):
        place_of = [raw.at[half * 3 + i, :, pl.ds(0, WIDTH)] for i in range(3)]
        return place_of + [pre.at[half, i] for i in range(2)]

    def local_loads(sources, pre):
        return [
            pltpu.make_async_copy(s, d, in_sem.at[len(small) + i])
            for i, (s, d) in enumerate(zip(sources, homes(0, pre)))
        ]

    def swaps(sources, pre):
        return [
            remote(s, d, swap_snd.at[i], swap_rcv.at[i], sibling)
            for i, (s, d) in enumerate(zip(sources, homes(1, pre)))
        ]

    def greet(dev):
        pl.semaphore_signal(barrier, inc=1, device_id=dev, device_id_type=MESH)

    barrier = pltpu.get_barrier_semaphore()

    @pl.when(core == 0)
    def _():
        for k in Z_STEPS[:7]:
            greet(at_z(k, 0)[1])
            greet(at_z(k, 1)[1])

    for c in loads:
        c.start()

    @pl.when(core == 0)
    def _():
        for k in Z_STEPS[7:]:
            greet(at_z(k, 0)[1])
            greet(at_z(k, 1)[1])

    for k in Y_STEPS:
        greet(at_y(k)[1])
    for k in X_STEPS:
        greet(at_x(k)[1])
    greet(sibling)

    @pl.when(core == 0)
    def _():
        for c in local_loads(routed_in, pre_r):
            c.start()

    @pl.when(core == 1)
    def _():
        for c in local_loads(shared_in, pre_s):
            c.start()

    for i in range(6):
        raw[i, :, WIDTH:] = jnp.zeros((HID, LANES), BF)
    for c in loads:
        c.wait()

    lane = lax.broadcasted_iota(jnp.int32, (LANES, FEAT), 0)
    feat = lax.broadcasted_iota(jnp.int32, (LANES, FEAT), 1)
    put_mine = (lane == feat + FEAT * core).astype(BF)
    mine = nn_dot(put_mine, x_mine[...]).T
    placed[0] = mine.astype(BF)
    expert_row = eidx[...]
    token_cap = jnp.zeros((1, TOK), jnp.int32)
    for e in range(NZ):
        token_cap = jnp.where(expert_row == e, cap[:, e : e + 1], token_cap)
    target = expert_row * 8 + slot[...]
    row_ids = lax.broadcasted_iota(jnp.int32, (NZ * 8, TOK), 0)
    placing = ((row_ids == target) & (slot[...] < token_cap)).astype(F32)
    eye = lax.broadcasted_iota(jnp.int32, (TOK, TOK), 0) == lax.broadcasted_iota(jnp.int32, (TOK, TOK), 1)
    share_col = jnp.sum(jnp.where(eye, share[...], 0.0), axis=1, keepdims=True)
    scaled = (share_col * mine).astype(BF)
    z_out[...] = nn_dot(placing.astype(BF), scaled).reshape(NZ, 8, LANES)

    pl.semaphore_wait(barrier, 1 + NY - 1 + NX - 1 + NZ - 1)

    pair = remote(placed.at[0], placed.at[1], pair_snd.at[0], pair_rcv.at[0], sibling)

    def send_slots(side):
        for k in Z_STEPS:
            zz, dev = at_z(k, 0)
            i = side * NZ + k
            remote(z_out.at[zz], z_in.at[side, z], z_snd.at[k], z_rcv.at[i], dev).start()

    def wait_slots(side, k):
        zz = lax.rem(z - k + NZ, NZ)
        i = side * NZ + k
        remote(z_out.at[zz], z_in.at[side, zz], z_snd.at[k], z_rcv.at[i], at_z(k, 0)[1]).wait_recv()

    def slots_sent():
        for k in range(1, NZ):
            zz, dev = at_z(k, 0)
            remote(z_out.at[zz], z_in.at[0, z], z_snd.at[k], z_rcv.at[k], dev).wait_send()

    pair_slots = remote(z_out.at[z], z_in.at[1, z], z_snd.at[0], z_rcv.at[NZ], sibling)

    def factors_r():
        g = jnp.concatenate([pre_r[0, 0], pre_r[1, 0]], axis=0)
        u = jnp.concatenate([pre_r[0, 1], pre_r[1, 1]], axis=0)
        a, b = silu_factors(g, u)
        factor_r[0], factor_r[1] = a.T, b.T

    def factors_s():
        for half in range(2):
            a, b = silu_factors(pre_s[half, 0], pre_s[half, 1])
            factor_s[0, :, half * HID : (half + 1) * HID] = a
            factor_s[1, :, half * HID : (half + 1) * HID] = b

    def silu_grads(grad_hidden, factor):
        return (grad_hidden * factor[0]).astype(BF), (grad_hidden * factor[1]).astype(BF)

    def window(i):
        half, kind = divmod(i, 3)
        for c in range(CHIPS):
            q, o = divmod(c * CHUNK, LANES)
            wide = raw[i, :, q * LANES : (q + 2) * LANES] if o else None
            piece = raw[i, :, q * LANES : (q + 1) * LANES] if o == 0 else wide[:, o : o + LANES]
            col = (c % NX) * LANES
            win[kind, c // NX, half * HID : (half + 1) * HID, col : col + LANES] = piece

    def send_y(rows):
        for k in Y_STEPS:
            remote(rows.at[y, x], rows.at[y, x], gy_snd.at[k], gy_rcv.at[k], at_y(k)[1]).start()

    def send_x(rows, k, yy):
        for j in X_STEPS:
            i = k * NX + j
            remote(rows.at[yy, x], rows.at[yy, x], gx_snd.at[i], gx_rcv.at[i], at_x(j)[1]).start()

    def relay_x(rows):
        send_x(rows, 0, y)
        for k in NEAR_FIRST:
            yy = lax.rem(y - k + NY, NY)
            remote(rows.at[yy, x], rows.at[yy, x], gy_snd.at[k], gy_rcv.at[k], at_y(k)[1]).wait_recv()
            send_x(rows, k, yy)

    def row_of(rows, k):
        yy = lax.rem(y - k + NY, NY)
        for j in X_STEPS:
            i = k * NX + j
            xx = lax.rem(x - j + NX, NX)
            remote(rows.at[yy, xx], rows.at[yy, xx], gx_snd.at[i], gx_rcv.at[i], at_x(j)[1]).wait_recv()
        return yy

    def hidden(rows):
        acc = None
        for k in (0,) + NEAR_FIRST:
            yy = row_of(rows, k)
            wide = jnp.concatenate([rows[yy, j] for j in range(NX)], axis=1)
            term = nt_dot(wide, win[0, yy])
            acc = term if acc is None else acc + term
        return acc

    def own_part(n, dg, du):
        for k in FAR_FIRST:
            yy = lax.rem(y + k, NY)
            t = nn_dot(dg, win[1, yy]) + nn_dot(du, win[2, yy])
            for j in range(NX):
                s = t[:, j * LANES : (j + 1) * LANES]
                four[j, 0:n] = s
                sums[yy, j, 0:n] = s.astype(BF)
            own[yy, 0:n] = four[x, 0:n]
            for j in X_STEPS:
                xx, dev = at_x(j)
                i = k * NX + j
                remote(
                    sums.at[yy, xx, pl.ds(0, n)], x_in.at[yy, j, pl.ds(0, n)],
                    rx_snd.at[i], rx_rcv.at[i], dev,
                ).start()

    def add_x(n, k):
        yy = lax.rem(y + k, NY)
        acc = own[yy, 0:n]
        for j in X_STEPS:
            i = k * NX + j
            remote(
                sums.at[yy, j, pl.ds(0, n)], x_in.at[yy, j, pl.ds(0, n)],
                rx_snd.at[i], rx_rcv.at[i], at_x(j)[1],
            ).wait_recv()
            acc += x_in[yy, j, 0:n].astype(F32)
        return acc

    def reduce(n):
        for k in FAR_FIRST[:-1]:
            y_out[k, 0:n] = add_x(n, k).astype(BF)
            remote(
                y_out.at[k, pl.ds(0, n)], y_in.at[k, pl.ds(0, n)], ry_snd.at[k], ry_rcv.at[k], at_y(k)[1]
            ).start()
        acc = add_x(n, 0)
        for k in NEAR_FIRST:
            remote(
                y_out.at[k, pl.ds(0, n)], y_in.at[k, pl.ds(0, n)], ry_snd.at[k], ry_rcv.at[k], at_y(k)[1]
            ).wait_recv()
            acc += y_in[k, 0:n].astype(F32)
        return acc

    def wait_sends(rows, n):
        for k in NEAR_FIRST:
            remote(rows.at[y, x], rows.at[y, x], gy_snd.at[k], gy_rcv.at[k], at_y(k)[1]).wait_send()
            remote(
                y_out.at[k, pl.ds(0, n)], y_in.at[k, pl.ds(0, n)], ry_snd.at[k], ry_rcv.at[k], at_y(k)[1]
            ).wait_send()
        for k in range(NY):
            for j in X_STEPS:
                i = k * NX + j
                remote(rows.at[y, x], rows.at[y, x], gx_snd.at[i], gx_rcv.at[i], at_x(j)[1]).wait_send()
                remote(
                    sums.at[k, j, pl.ds(0, n)], x_in.at[k, j, pl.ds(0, n)],
                    rx_snd.at[i], rx_rcv.at[i], at_x(j)[1],
                ).wait_send()

    answer = remote(shared_sum.at[0], shared_sum.at[1], pair_snd.at[1], pair_rcv.at[1], sibling)
    pair_back = remote(z2_out.at[z], z2_in.at[z], z2_snd.at[NZ], z2_rcv.at[0], sibling)

    def wait_back(k, side):
        zz = lax.rem(z - k + NZ, NZ)
        i = side * NZ + k
        remote(z2_out.at[zz], z2_in.at[zz], z2_snd.at[i], z2_rcv.at[k], at_z(k, side)[1]).wait_recv()

    def token_rows():
        back = z2_in[...].reshape(NZ * 8, LANES)
        return lax.dot_general(
            place[...], back, (((1,), (0,)), ((), ())),
            precision=lax.Precision.HIGHEST, preferred_element_type=F32,
        )

    @pl.when(core == 0)
    def _():
        send_slots(0)
        pair.start()
        for c in swaps(shared_in, pre_s):
            c.start()
        z_in[0, z] = z_out[z]
        place[...] = placing.T
        z2_out[...] = jnp.zeros_like(z2_out)
        loaded = local_loads(routed_in, pre_r)
        for i in range(5):
            loaded[i].wait()
        for i in range(3):
            window(i)
        pair_slots.wait_recv()
        for k in range(1, NZ):
            wait_slots(0, k)
            wait_slots(1, k)
        for b in range(NZ):
            slots[b * CAP : (b + 1) * CAP] = z_in[0, b, 0:CAP] + z_in[1, b, 0:CAP]
        rows_r[y, x] = slots[...].astype(BF)
        send_y(rows_r)
        relay_x(rows_r)
        arrive = swaps(routed_in, pre_r)
        arrive[3].wait_recv()
        arrive[4].wait_recv()
        factors_r()
        for i in range(3):
            arrive[i].wait_recv()
            window(3 + i)
        dg, du = silu_grads(hidden(rows_r), factor_r)
        own_part(ROUTED, dg, du)
        slots[...] = reduce(ROUTED)
        for b in range(NZ):
            z2_out[b, 0:CAP] = slots[b * CAP : (b + 1) * CAP]
        for k in Z_STEPS:
            for side in range(2):
                zz, dev = at_z(k, side)
                i = side * NZ + k
                remote(z2_out.at[zz], z2_in.at[z], z2_snd.at[i], z2_rcv.at[k], dev).start()
        pair_back.start()
        z2_in[z] = z2_out[z]
        wait_sends(rows_r, ROUTED)
        for c in swaps(shared_in, pre_s):
            c.wait_send()
        slots_sent()
        pair.wait_send()
        answer.wait_recv()
        for k in range(1, NZ):
            wait_back(k, 0)
        out_ref[...] = (shared_sum[1] + token_rows()).T[0:FEAT].astype(BF)
        for k in range(1, NZ):
            for side in range(2):
                zz, dev = at_z(k, side)
                i = side * NZ + k
                remote(z2_out.at[zz], z2_in.at[z], z2_snd.at[i], z2_rcv.at[k], dev).wait_send()
        pair_back.wait_send()

    @pl.when(core == 1)
    def _():
        send_slots(1)
        pair_slots.start()
        pair.wait_recv()
        rows_s[y, x] = placed[0] + placed[1]
        send_y(rows_s)
        for c in swaps(routed_in, pre_r):
            c.start()
        place[...] = placing.T
        loaded = local_loads(shared_in, pre_s)
        for i in range(5):
            loaded[i].wait()
        for i in range(3):
            window(i)
        relay_x(rows_s)
        arrive = swaps(shared_in, pre_s)
        arrive[3].wait_recv()
        arrive[4].wait_recv()
        factors_s()
        for i in range(3):
            arrive[i].wait_recv()
            window(3 + i)
        dg, du = silu_grads(hidden(rows_s), factor_s)
        own_part(TOK, dg, du)
        shared_sum[0] = reduce(TOK)
        answer.start()
        wait_sends(rows_s, TOK)
        for c in swaps(routed_in, pre_r):
            c.wait_send()
        slots_sent()
        pair_slots.wait_send()
        answer.wait_send()
        pair_back.wait_recv()
        for k in range(1, NZ):
            wait_back(k, 1)
        out_ref[...] = (shared_sum[0] + token_rows()).T[FEAT:CHUNK].astype(BF)


def body(
    grad_out, expert_index, slot_index, capacity, router_share,
    routed_gate, routed_up, gate_weight, up_weight, down_weight,
    shared_gate, shared_up, gate_common, up_common, down_common,
):
    dma = pltpu.SemaphoreType.DMA
    scratch = [
        pltpu.VMEM((FEAT, TOK), BF),
        pltpu.VMEM((1, TOK), jnp.int32), pltpu.VMEM((1, TOK), jnp.int32),
        pltpu.VMEM((1, NZ), jnp.int32), pltpu.VMEM((1, TOK), F32),
        pltpu.VMEM((2, 2, HID, ROUTED), BF), pltpu.VMEM((2, 2, TOK, HID), BF),
        pltpu.VMEM((2, ROUTED, 2 * HID), F32), pltpu.VMEM((2, TOK, 2 * HID), F32), pltpu.VMEM((2, TOK, LANES), BF),
        pltpu.VMEM((6, HID, WIDTH + LANES), BF),
        pltpu.VMEM((3, NY, 2 * HID, NX * LANES), BF),
        pltpu.VMEM((TOK, NZ * 8), F32),
        pltpu.VMEM((NZ, 8, LANES), F32), pltpu.VMEM((2, NZ, 8, LANES), F32),
        pltpu.VMEM((NZ, 8, LANES), F32), pltpu.VMEM((NZ, 8, LANES), F32),
        pltpu.VMEM((ROUTED, LANES), F32),
        pltpu.VMEM((NY, NX, ROUTED, LANES), BF), pltpu.VMEM((NY, NX, TOK, LANES), BF),
        pltpu.VMEM((NX, ROUTED, LANES), F32), pltpu.VMEM((NY, ROUTED, LANES), F32),
        pltpu.VMEM((NY, NX, ROUTED, LANES), BF), pltpu.VMEM((NY, NX, ROUTED, LANES), BF),
        pltpu.VMEM((NY, ROUTED, LANES), BF), pltpu.VMEM((NY, ROUTED, LANES), BF),
        pltpu.VMEM((2, TOK, LANES), F32),
        dma((10,)), dma((2,)), dma((2,)), dma((NZ,)), dma((2 * NZ,)), dma((2 * NZ,)), dma((NZ,)),
        dma((NY,)), dma((NY,)), dma((NY * NX,)), dma((NY * NX,)), dma((5,)), dma((5,)),
        dma((NY * NX,)), dma((NY * NX,)), dma((NY,)), dma((NY,)),
    ]
    out = pl.pallas_call(
        kernel,
        out_shape=jax.ShapeDtypeStruct((FEAT, TOK), BF),
        in_specs=[pl.BlockSpec(memory_space=pl.ANY)] * 15,
        out_specs=pl.BlockSpec(memory_space=pltpu.VMEM),
        scratch_shapes=scratch,
        compiler_params=pltpu.CompilerParams(
            collective_id=0, has_side_effects=True, vmem_limit_bytes=56 * 1024 * 1024
        ),
    )(
        grad_out.T, expert_index.reshape(1, -1), slot_index.reshape(1, -1), capacity.reshape(1, -1),
        router_share.reshape(1, -1), routed_gate.swapaxes(1, 2), routed_up.swapaxes(1, 2), gate_weight, up_weight, down_weight,
        shared_gate, shared_up, gate_common, up_common, down_common,
    )
    return out.T


def solution(mesh):
    return jax.shard_map(
        body,
        mesh=mesh,
        in_specs=(
            P("expert", "dp"), P("expert"), P("expert"), P(), P("expert"),
            P("expert", None, "dp"), P("expert", None, "dp"),
            P("expert", "dp", None), P("expert", "dp", None), P("expert", "dp", None),
            P("expert", "dp"), P("expert", "dp"),
            P("dp", None), P("dp", None), P("dp", None),
        ),
        out_specs=P("expert", "dp"),
        check_vma=False,
    )
```

```python
import jax
import jax.numpy as jnp
from jax import lax
from jax.experimental import pallas as pl
from jax.experimental.pallas import tpu as pltpu
from jax.sharding import PartitionSpec as P

BF = jnp.bfloat16
F32 = jnp.float32
MESH = pl.DeviceIdType.MESH
NX, NY, NZ = 4, 8, 16
CHIPS = NX * NY
TOK = 64
CAP = 5
ROUTED = NZ * CAP
HID = 144
FEAT = 50
CHUNK = 2 * FEAT
LANES = 128
WIDTH = CHIPS * CHUNK
NEAR_FIRST = (1, 7, 2, 6, 3, 5, 4)
FAR_FIRST = (4, 3, 5, 2, 6, 1, 7, 0)
X_STEPS = (2, 1, 3)
Y_STEPS = (4, 3, 5, 2, 6, 1, 7)
Z_STEPS = (8, 7, 9, 6, 10, 5, 11, 4, 12, 3, 13, 2, 14, 1, 15)


def nt_dot(a, b):
    return lax.dot_general(a, b, (((1,), (1,)), ((), ())), preferred_element_type=F32)


def nn_dot(a, b):
    return lax.dot_general(a, b, (((1,), (0,)), ((), ())), preferred_element_type=F32)


def silu_factors(gate_pre, up_pre):
    g = gate_pre.astype(F32)
    u = up_pre.astype(F32)
    s = 1.0 / (1.0 + jnp.exp(-g))
    return u * s * (1.0 + g * (1.0 - s)), g * s


def kernel(
    x_hbm, eidx_hbm, slot_hbm, cap_hbm, share_hbm,
    rg_hbm, ru_hbm, gw_hbm, uw_hbm, dw_hbm,
    sg_hbm, su_hbm, gc_hbm, uc_hbm, dc_hbm,
    out_ref,
    x_mine, eidx, slot, cap, share,
    pre_r, pre_s, factor_r, factor_s, placed,
    raw, win, place,
    z_out, z_in, z2_out, z2_in, slots,
    rows_r, rows_s,
    four, own, sums, x_in, y_out, y_in,
    shared_sum,
    in_sem, pair_snd, pair_rcv, z_snd, z_rcv, z2_snd, z2_rcv,
    gy_snd, gy_rcv, gx_snd, gx_rcv, swap_snd, swap_rcv, rx_snd, rx_rcv, ry_snd, ry_rcv,
):
    dp = lax.axis_index("dp")
    z = lax.axis_index("expert")
    core = lax.rem(dp, 2)
    chip = dp // 2
    x = lax.rem(chip, NX)
    y = chip // NX

    def at_y(k):
        yy = lax.rem(y + k, NY)
        return yy, ((yy * NX + x) * 2 + core, z)

    def at_x(k):
        xx = lax.rem(x + k, NX)
        return xx, ((y * NX + xx) * 2 + core, z)

    def at_z(k, side):
        zz = lax.rem(z + k, NZ)
        return zz, (chip * 2 + side, zz)

    sibling = (chip * 2 + 1 - core, z)

    def remote(src, dst, snd, rcv, dev):
        return pltpu.make_async_remote_copy(
            src_ref=src, dst_ref=dst, send_sem=snd, recv_sem=rcv, device_id=dev, device_id_type=MESH
        )

    small = ((x_hbm, x_mine), (eidx_hbm, eidx), (slot_hbm, slot), (cap_hbm, cap), (share_hbm, share))
    loads = [pltpu.make_async_copy(s, d, in_sem.at[i]) for i, (s, d) in enumerate(small)]
    routed_in = (dw_hbm.at[0], gw_hbm.at[0], uw_hbm.at[0], rg_hbm.at[0], ru_hbm.at[0])
    shared_in = (dc_hbm, gc_hbm, uc_hbm, sg_hbm, su_hbm)

    def homes(half, pre):
        place_of = [raw.at[half * 3 + i, :, pl.ds(0, WIDTH)] for i in range(3)]
        return place_of + [pre.at[half, i] for i in range(2)]

    def local_loads(sources, pre):
        return [
            pltpu.make_async_copy(s, d, in_sem.at[len(small) + i])
            for i, (s, d) in enumerate(zip(sources, homes(0, pre)))
        ]

    def swaps(sources, pre):
        return [
            remote(s, d, swap_snd.at[i], swap_rcv.at[i], sibling)
            for i, (s, d) in enumerate(zip(sources, homes(1, pre)))
        ]

    def greet(dev):
        pl.semaphore_signal(barrier, inc=1, device_id=dev, device_id_type=MESH)

    barrier = pltpu.get_barrier_semaphore()

    for c in loads:
        c.start()

    def greet_z(steps):
        @pl.when(core == 0)
        def _():
            for k in steps:
                greet(at_z(k, 0)[1])
                greet(at_z(k, 1)[1])

    greet_z(Z_STEPS[:7])
    greet(at_y(4)[1])
    greet_z(Z_STEPS[7:9])
    for k in Y_STEPS[1:3]:
        greet(at_y(k)[1])
    greet_z(Z_STEPS[9:11])
    greet(at_x(2)[1])
    for k in Y_STEPS[3:5]:
        greet(at_y(k)[1])
    greet_z(Z_STEPS[11:13])
    for k in Y_STEPS[5:]:
        greet(at_y(k)[1])
    for k in X_STEPS[1:]:
        greet(at_x(k)[1])
    greet_z(Z_STEPS[13:])
    greet(sibling)

    @pl.when(core == 0)
    def _():
        for c in local_loads(routed_in, pre_r):
            c.start()

    @pl.when(core == 1)
    def _():
        for c in local_loads(shared_in, pre_s):
            c.start()

    for i in range(6):
        raw[i, :, WIDTH:] = jnp.zeros((HID, LANES), BF)
    for c in loads:
        c.wait()

    lane = lax.broadcasted_iota(jnp.int32, (LANES, FEAT), 0)
    feat = lax.broadcasted_iota(jnp.int32, (LANES, FEAT), 1)
    put_mine = (lane == feat + FEAT * core).astype(BF)
    mine = nn_dot(put_mine, x_mine[...]).T
    placed[0] = mine.astype(BF)
    expert_row = eidx[...]
    token_cap = jnp.zeros((1, TOK), jnp.int32)
    for e in range(NZ):
        token_cap = jnp.where(expert_row == e, cap[:, e : e + 1], token_cap)
    target = expert_row * 8 + slot[...]
    row_ids = lax.broadcasted_iota(jnp.int32, (NZ * 8, TOK), 0)
    placing = ((row_ids == target) & (slot[...] < token_cap)).astype(F32)
    eye = lax.broadcasted_iota(jnp.int32, (TOK, TOK), 0) == lax.broadcasted_iota(jnp.int32, (TOK, TOK), 1)
    share_col = jnp.sum(jnp.where(eye, share[...], 0.0), axis=1, keepdims=True)
    scaled = (share_col * mine).astype(BF)
    z_out[...] = nn_dot(placing.astype(BF), scaled).reshape(NZ, 8, LANES)

    pl.semaphore_wait(barrier, 1 + NY - 1 + NX - 1 + NZ - 1)

    pair = remote(placed.at[0], placed.at[1], pair_snd.at[0], pair_rcv.at[0], sibling)

    def send_slots(side):
        for k in Z_STEPS:
            zz, dev = at_z(k, 0)
            i = side * NZ + k
            remote(z_out.at[zz], z_in.at[side, z], z_snd.at[k], z_rcv.at[i], dev).start()

    def wait_slots(side, k):
        zz = lax.rem(z - k + NZ, NZ)
        i = side * NZ + k
        remote(z_out.at[zz], z_in.at[side, zz], z_snd.at[k], z_rcv.at[i], at_z(k, 0)[1]).wait_recv()

    def slots_sent():
        for k in range(1, NZ):
            zz, dev = at_z(k, 0)
            remote(z_out.at[zz], z_in.at[0, z], z_snd.at[k], z_rcv.at[k], dev).wait_send()

    pair_slots = remote(z_out.at[z], z_in.at[1, z], z_snd.at[0], z_rcv.at[NZ], sibling)

    def factors_r():
        g = jnp.concatenate([pre_r[0, 0], pre_r[1, 0]], axis=0)
        u = jnp.concatenate([pre_r[0, 1], pre_r[1, 1]], axis=0)
        a, b = silu_factors(g, u)
        factor_r[0], factor_r[1] = a.T, b.T

    def factors_s():
        for half in range(2):
            a, b = silu_factors(pre_s[half, 0], pre_s[half, 1])
            factor_s[0, :, half * HID : (half + 1) * HID] = a
            factor_s[1, :, half * HID : (half + 1) * HID] = b

    def silu_grads(grad_hidden, factor):
        return (grad_hidden * factor[0]).astype(BF), (grad_hidden * factor[1]).astype(BF)

    def window(i):
        half, kind = divmod(i, 3)
        for c in range(CHIPS):
            q, o = divmod(c * CHUNK, LANES)
            wide = raw[i, :, q * LANES : (q + 2) * LANES] if o else None
            piece = raw[i, :, q * LANES : (q + 1) * LANES] if o == 0 else wide[:, o : o + LANES]
            col = (c % NX) * LANES
            win[kind, c // NX, half * HID : (half + 1) * HID, col : col + LANES] = piece

    def send_y(rows):
        for k in NEAR_FIRST:
            remote(rows.at[y, x], rows.at[y, x], gy_snd.at[k], gy_rcv.at[k], at_y(k)[1]).start()

    def send_x(rows, k, yy):
        for j in X_STEPS:
            i = k * NX + j
            remote(rows.at[yy, x], rows.at[yy, x], gx_snd.at[i], gx_rcv.at[i], at_x(j)[1]).start()

    def relay_x(rows):
        send_x(rows, 0, y)
        for k in NEAR_FIRST:
            yy = lax.rem(y - k + NY, NY)
            remote(rows.at[yy, x], rows.at[yy, x], gy_snd.at[k], gy_rcv.at[k], at_y(k)[1]).wait_recv()
            send_x(rows, k, yy)

    def row_of(rows, k):
        yy = lax.rem(y - k + NY, NY)
        for j in X_STEPS:
            i = k * NX + j
            xx = lax.rem(x - j + NX, NX)
            remote(rows.at[yy, xx], rows.at[yy, xx], gx_snd.at[i], gx_rcv.at[i], at_x(j)[1]).wait_recv()
        return yy

    def hidden(rows):
        acc = None
        for k in (0,) + NEAR_FIRST:
            yy = row_of(rows, k)
            wide = jnp.concatenate([rows[yy, j] for j in range(NX)], axis=1)
            term = nt_dot(wide, win[0, yy])
            acc = term if acc is None else acc + term
        return acc

    def own_part(n, dg, du):
        for k in FAR_FIRST:
            yy = lax.rem(y + k, NY)
            t = nn_dot(dg, win[1, yy]) + nn_dot(du, win[2, yy])
            for j in range(NX):
                s = t[:, j * LANES : (j + 1) * LANES]
                four[j, 0:n] = s
                sums[yy, j, 0:n] = s.astype(BF)
            own[yy, 0:n] = four[x, 0:n]
            for j in X_STEPS:
                xx, dev = at_x(j)
                i = k * NX + j
                remote(
                    sums.at[yy, xx, pl.ds(0, n)], x_in.at[yy, j, pl.ds(0, n)],
                    rx_snd.at[i], rx_rcv.at[i], dev,
                ).start()

    def add_x(n, k):
        yy = lax.rem(y + k, NY)
        acc = own[yy, 0:n]
        for j in X_STEPS:
            i = k * NX + j
            remote(
                sums.at[yy, j, pl.ds(0, n)], x_in.at[yy, j, pl.ds(0, n)],
                rx_snd.at[i], rx_rcv.at[i], at_x(j)[1],
            ).wait_recv()
            acc += x_in[yy, j, 0:n].astype(F32)
        return acc

    def reduce(n):
        for k in FAR_FIRST[:-1]:
            y_out[k, 0:n] = add_x(n, k).astype(BF)
            remote(
                y_out.at[k, pl.ds(0, n)], y_in.at[k, pl.ds(0, n)], ry_snd.at[k], ry_rcv.at[k], at_y(k)[1]
            ).start()
        acc = add_x(n, 0)
        for k in NEAR_FIRST:
            remote(
                y_out.at[k, pl.ds(0, n)], y_in.at[k, pl.ds(0, n)], ry_snd.at[k], ry_rcv.at[k], at_y(k)[1]
            ).wait_recv()
            acc += y_in[k, 0:n].astype(F32)
        return acc

    def wait_sends(rows, n):
        for k in NEAR_FIRST:
            remote(rows.at[y, x], rows.at[y, x], gy_snd.at[k], gy_rcv.at[k], at_y(k)[1]).wait_send()
            remote(
                y_out.at[k, pl.ds(0, n)], y_in.at[k, pl.ds(0, n)], ry_snd.at[k], ry_rcv.at[k], at_y(k)[1]
            ).wait_send()
        for k in range(NY):
            for j in X_STEPS:
                i = k * NX + j
                remote(rows.at[y, x], rows.at[y, x], gx_snd.at[i], gx_rcv.at[i], at_x(j)[1]).wait_send()
                remote(
                    sums.at[k, j, pl.ds(0, n)], x_in.at[k, j, pl.ds(0, n)],
                    rx_snd.at[i], rx_rcv.at[i], at_x(j)[1],
                ).wait_send()

    answer = remote(shared_sum.at[0], shared_sum.at[1], pair_snd.at[1], pair_rcv.at[1], sibling)
    pair_back = remote(z2_out.at[z], z2_in.at[z], z2_snd.at[NZ], z2_rcv.at[0], sibling)

    def wait_back(k, side):
        zz = lax.rem(z - k + NZ, NZ)
        i = side * NZ + k
        remote(z2_out.at[zz], z2_in.at[zz], z2_snd.at[i], z2_rcv.at[k], at_z(k, side)[1]).wait_recv()

    def token_rows():
        back = z2_in[...].reshape(NZ * 8, LANES)
        high = back.astype(BF)
        low = (back - high.astype(F32)).astype(BF)
        return nn_dot(place[...], high) + nn_dot(place[...], low)

    @pl.when(core == 0)
    def _():
        send_slots(0)
        pair.start()
        for c in swaps(shared_in, pre_s):
            c.start()
        z_in[0, z] = z_out[z]
        place[...] = placing.T.astype(BF)
        z2_out[...] = jnp.zeros_like(z2_out)
        loaded = local_loads(routed_in, pre_r)
        for i in range(5):
            loaded[i].wait()
        for i in range(3):
            window(i)
        pair_slots.wait_recv()
        for k in Z_STEPS[::-1]:
            wait_slots(0, k)
            wait_slots(1, k)
        for b in range(NZ):
            slots[b * CAP : (b + 1) * CAP] = z_in[0, b, 0:CAP] + z_in[1, b, 0:CAP]
        rows_r[y, x] = slots[...].astype(BF)
        send_y(rows_r)
        arrive = swaps(routed_in, pre_r)
        arrive[3].wait_recv()
        arrive[4].wait_recv()
        factors_r()
        for i in range(3):
            arrive[i].wait_recv()
            window(3 + i)
        relay_x(rows_r)
        dg, du = silu_grads(hidden(rows_r), factor_r)
        own_part(ROUTED, dg, du)
        slots[...] = reduce(ROUTED)
        for b in range(NZ):
            z2_out[b, 0:CAP] = slots[b * CAP : (b + 1) * CAP]
        for k in Z_STEPS:
            for side in range(2):
                zz, dev = at_z(k, side)
                i = side * NZ + k
                remote(z2_out.at[zz], z2_in.at[z], z2_snd.at[i], z2_rcv.at[k], dev).start()
        pair_back.start()
        z2_in[z] = z2_out[z]
        wait_sends(rows_r, ROUTED)
        for c in swaps(shared_in, pre_s):
            c.wait_send()
        slots_sent()
        pair.wait_send()
        answer.wait_recv()
        for k in Z_STEPS[::-1]:
            wait_back(k, 0)
        out_ref[...] = (shared_sum[1] + token_rows()).T[0:FEAT].astype(BF)
        for k in range(1, NZ):
            for side in range(2):
                zz, dev = at_z(k, side)
                i = side * NZ + k
                remote(z2_out.at[zz], z2_in.at[z], z2_snd.at[i], z2_rcv.at[k], dev).wait_send()
        pair_back.wait_send()

    @pl.when(core == 1)
    def _():
        send_slots(1)
        pair_slots.start()
        pair.wait_recv()
        rows_s[y, x] = placed[0] + placed[1]
        send_y(rows_s)
        for c in swaps(routed_in, pre_r):
            c.start()
        place[...] = placing.T.astype(BF)
        loaded = local_loads(shared_in, pre_s)
        for i in range(5):
            loaded[i].wait()
        for i in range(3):
            window(i)
        relay_x(rows_s)
        arrive = swaps(shared_in, pre_s)
        arrive[3].wait_recv()
        arrive[4].wait_recv()
        factors_s()
        for i in range(3):
            arrive[i].wait_recv()
            window(3 + i)
        dg, du = silu_grads(hidden(rows_s), factor_s)
        own_part(TOK, dg, du)
        shared_sum[0] = reduce(TOK)
        answer.start()
        wait_sends(rows_s, TOK)
        for c in swaps(routed_in, pre_r):
            c.wait_send()
        slots_sent()
        pair_slots.wait_send()
        answer.wait_send()
        pair_back.wait_recv()
        for k in Z_STEPS[::-1]:
            wait_back(k, 1)
        out_ref[...] = (shared_sum[0] + token_rows()).T[FEAT:CHUNK].astype(BF)


def body(
    grad_out, expert_index, slot_index, capacity, router_share,
    routed_gate, routed_up, gate_weight, up_weight, down_weight,
    shared_gate, shared_up, gate_common, up_common, down_common,
):
    dma = pltpu.SemaphoreType.DMA
    scratch = [
        pltpu.VMEM((FEAT, TOK), BF),
        pltpu.VMEM((1, TOK), jnp.int32), pltpu.VMEM((1, TOK), jnp.int32),
        pltpu.VMEM((1, NZ), jnp.int32), pltpu.VMEM((1, TOK), F32),
        pltpu.VMEM((2, 2, HID, ROUTED), BF), pltpu.VMEM((2, 2, TOK, HID), BF),
        pltpu.VMEM((2, ROUTED, 2 * HID), F32), pltpu.VMEM((2, TOK, 2 * HID), F32), pltpu.VMEM((2, TOK, LANES), BF),
        pltpu.VMEM((6, HID, WIDTH + LANES), BF),
        pltpu.VMEM((3, NY, 2 * HID, NX * LANES), BF),
        pltpu.VMEM((TOK, NZ * 8), BF),
        pltpu.VMEM((NZ, 8, LANES), F32), pltpu.VMEM((2, NZ, 8, LANES), F32),
        pltpu.VMEM((NZ, 8, LANES), F32), pltpu.VMEM((NZ, 8, LANES), F32),
        pltpu.VMEM((ROUTED, LANES), F32),
        pltpu.VMEM((NY, NX, ROUTED, LANES), BF), pltpu.VMEM((NY, NX, TOK, LANES), BF),
        pltpu.VMEM((NX, ROUTED, LANES), F32), pltpu.VMEM((NY, ROUTED, LANES), F32),
        pltpu.VMEM((NY, NX, ROUTED, LANES), BF), pltpu.VMEM((NY, NX, ROUTED, LANES), BF),
        pltpu.VMEM((NY, ROUTED, LANES), BF), pltpu.VMEM((NY, ROUTED, LANES), BF),
        pltpu.VMEM((2, TOK, LANES), F32),
        dma((10,)), dma((2,)), dma((2,)), dma((NZ,)), dma((2 * NZ,)), dma((2 * NZ,)), dma((NZ,)),
        dma((NY,)), dma((NY,)), dma((NY * NX,)), dma((NY * NX,)), dma((5,)), dma((5,)),
        dma((NY * NX,)), dma((NY * NX,)), dma((NY,)), dma((NY,)),
    ]
    out = pl.pallas_call(
        kernel,
        out_shape=jax.ShapeDtypeStruct((FEAT, TOK), BF),
        in_specs=[pl.BlockSpec(memory_space=pl.ANY)] * 15,
        out_specs=pl.BlockSpec(memory_space=pltpu.VMEM),
        scratch_shapes=scratch,
        compiler_params=pltpu.CompilerParams(
            collective_id=0, has_side_effects=True, vmem_limit_bytes=56 * 1024 * 1024
        ),
    )(
        grad_out.T, expert_index.reshape(1, -1), slot_index.reshape(1, -1), capacity.reshape(1, -1),
        router_share.reshape(1, -1), routed_gate.swapaxes(1, 2), routed_up.swapaxes(1, 2), gate_weight, up_weight, down_weight,
        shared_gate, shared_up, gate_common, up_common, down_common,
    )
    return out.T


def solution(mesh):
    return jax.shard_map(
        body,
        mesh=mesh,
        in_specs=(
            P("expert", "dp"), P("expert"), P("expert"), P(), P("expert"),
            P("expert", None, "dp"), P("expert", None, "dp"),
            P("expert", "dp", None), P("expert", "dp", None), P("expert", "dp", None),
            P("expert", "dp"), P("expert", "dp"),
            P("dp", None), P("dp", None), P("dp", None),
        ),
        out_specs=P("expert", "dp"),
        check_vma=False,
    )
```

```python
import jax
import jax.numpy as jnp
from jax import lax
from jax.experimental import pallas as pl
from jax.experimental.pallas import tpu as pltpu
from jax.sharding import PartitionSpec as P

BF = jnp.bfloat16
F32 = jnp.float32
MESH = pl.DeviceIdType.MESH
NX, NY, NZ = 4, 8, 16
CHIPS = NX * NY
TOK = 64
CAP = 5
ROUTED = NZ * CAP
HID = 144
FEAT = 50
CHUNK = 2 * FEAT
LANES = 128
WIDTH = CHIPS * CHUNK
NEAR_FIRST = (1, 7, 2, 6, 3, 5, 4)
SLOTS = (0,) + NEAR_FIRST
BATCHES = ((0, 1), (1, 2), (3, 2), (5, 3))
FAR_FIRST = (4, 3, 5, 2, 6, 1, 7, 0)
X_STEPS = (2, 1, 3)
Y_STEPS = (4, 3, 5, 2, 6, 1, 7)
Z_STEPS = (8, 7, 9, 6, 10, 5, 11, 4, 12, 3, 13, 2, 14, 1, 15)


def nt_dot(a, b):
    return lax.dot_general(a, b, (((1,), (1,)), ((), ())), preferred_element_type=F32)


def nn_dot(a, b):
    return lax.dot_general(a, b, (((1,), (0,)), ((), ())), preferred_element_type=F32)


def silu_factors(gate_pre, up_pre):
    g = gate_pre.astype(F32)
    u = up_pre.astype(F32)
    s = 1.0 / (1.0 + jnp.exp(-g))
    return u * s * (1.0 + g * (1.0 - s)), g * s


def kernel(
    x_hbm, eidx_hbm, slot_hbm, cap_hbm, share_hbm,
    rg_hbm, ru_hbm, gw_hbm, uw_hbm, dw_hbm,
    sg_hbm, su_hbm, gc_hbm, uc_hbm, dc_hbm,
    out_ref,
    x_mine, eidx, slot, cap, share,
    pre_r, pre_s, factor_r, factor_s, placed,
    raw, win, place,
    z_out, z_in, z2_out, z2_in, slots,
    rows_r, rows_s,
    four, own, sums, x_in, y_out, y_in,
    shared_sum,
    in_sem, pair_snd, pair_rcv, z_snd, z_rcv, z2_snd, z2_rcv,
    gy_snd, gy_rcv, gx_snd, gx_rcv, swap_snd, swap_rcv, rx_snd, rx_rcv, ry_snd, ry_rcv,
):
    dp = lax.axis_index("dp")
    z = lax.axis_index("expert")
    core = lax.rem(dp, 2)
    chip = dp // 2
    x = lax.rem(chip, NX)
    y = chip // NX

    def at_y(k):
        yy = lax.rem(y + k, NY)
        return yy, ((yy * NX + x) * 2 + core, z)

    def at_x(k):
        xx = lax.rem(x + k, NX)
        return xx, ((y * NX + xx) * 2 + core, z)

    def at_z(k, side):
        zz = lax.rem(z + k, NZ)
        return zz, (chip * 2 + side, zz)

    sibling = (chip * 2 + 1 - core, z)

    def remote(src, dst, snd, rcv, dev):
        return pltpu.make_async_remote_copy(
            src_ref=src, dst_ref=dst, send_sem=snd, recv_sem=rcv, device_id=dev, device_id_type=MESH
        )

    small = ((x_hbm, x_mine), (eidx_hbm, eidx), (slot_hbm, slot), (cap_hbm, cap), (share_hbm, share))
    loads = [pltpu.make_async_copy(s, d, in_sem.at[i]) for i, (s, d) in enumerate(small)]
    routed_in = (dw_hbm.at[0], gw_hbm.at[0], uw_hbm.at[0], rg_hbm.at[0], ru_hbm.at[0])
    shared_in = (dc_hbm, gc_hbm, uc_hbm, sg_hbm, su_hbm)

    def homes(half, pre):
        place_of = [raw.at[half * 3 + i, :, pl.ds(0, WIDTH)] for i in range(3)]
        return place_of + [pre.at[half, i] for i in range(2)]

    def local_loads(sources, pre):
        return [
            pltpu.make_async_copy(s, d, in_sem.at[len(small) + i])
            for i, (s, d) in enumerate(zip(sources, homes(0, pre)))
        ]

    def swaps(sources, pre):
        return [
            remote(s, d, swap_snd.at[i], swap_rcv.at[i], sibling)
            for i, (s, d) in enumerate(zip(sources, homes(1, pre)))
        ]

    def greet(dev):
        pl.semaphore_signal(barrier, inc=1, device_id=dev, device_id_type=MESH)

    barrier = pltpu.get_barrier_semaphore()

    for c in loads:
        c.start()

    def greet_z(steps):
        @pl.when(core == 0)
        def _():
            for k in steps:
                greet(at_z(k, 0)[1])
                greet(at_z(k, 1)[1])

    greet_z(Z_STEPS[:7])
    greet(at_y(4)[1])
    greet_z(Z_STEPS[7:9])
    for k in Y_STEPS[1:3]:
        greet(at_y(k)[1])
    greet_z(Z_STEPS[9:11])
    greet(at_x(2)[1])
    for k in Y_STEPS[3:5]:
        greet(at_y(k)[1])
    greet_z(Z_STEPS[11:13])
    for k in Y_STEPS[5:]:
        greet(at_y(k)[1])
    for k in X_STEPS[1:]:
        greet(at_x(k)[1])
    greet_z(Z_STEPS[13:])
    greet(sibling)

    @pl.when(core == 0)
    def _():
        for c in local_loads(routed_in, pre_r):
            c.start()

    @pl.when(core == 1)
    def _():
        for c in local_loads(shared_in, pre_s):
            c.start()

    for i in range(6):
        raw[i, :, WIDTH:] = jnp.zeros((HID, LANES), BF)
    for c in loads:
        c.wait()

    lane = lax.broadcasted_iota(jnp.int32, (LANES, FEAT), 0)
    feat = lax.broadcasted_iota(jnp.int32, (LANES, FEAT), 1)
    put_mine = (lane == feat + FEAT * core).astype(BF)
    mine = nn_dot(put_mine, x_mine[...]).T
    placed[0] = mine.astype(BF)
    expert_row = eidx[...]
    token_cap = jnp.zeros((1, TOK), jnp.int32)
    for e in range(NZ):
        token_cap = jnp.where(expert_row == e, cap[:, e : e + 1], token_cap)
    target = expert_row * 8 + slot[...]
    row_ids = lax.broadcasted_iota(jnp.int32, (NZ * 8, TOK), 0)
    placing = ((row_ids == target) & (slot[...] < token_cap)).astype(F32)
    eye = lax.broadcasted_iota(jnp.int32, (TOK, TOK), 0) == lax.broadcasted_iota(jnp.int32, (TOK, TOK), 1)
    share_col = jnp.sum(jnp.where(eye, share[...], 0.0), axis=1, keepdims=True)
    scaled = (share_col * mine).astype(BF)
    z_out[...] = nn_dot(placing.astype(BF), scaled).reshape(NZ, 8, LANES)

    pl.semaphore_wait(barrier, 1 + NY - 1 + NX - 1 + NZ - 1)

    pair = remote(placed.at[0], placed.at[1], pair_snd.at[0], pair_rcv.at[0], sibling)

    def send_slots(side):
        for k in Z_STEPS:
            zz, dev = at_z(k, 0)
            i = side * NZ + k
            remote(z_out.at[zz], z_in.at[side, z], z_snd.at[k], z_rcv.at[i], dev).start()

    def wait_slots(side, k):
        zz = lax.rem(z - k + NZ, NZ)
        i = side * NZ + k
        remote(z_out.at[zz], z_in.at[side, zz], z_snd.at[k], z_rcv.at[i], at_z(k, 0)[1]).wait_recv()

    def slots_sent():
        for k in range(1, NZ):
            zz, dev = at_z(k, 0)
            remote(z_out.at[zz], z_in.at[0, z], z_snd.at[k], z_rcv.at[k], dev).wait_send()

    pair_slots = remote(z_out.at[z], z_in.at[1, z], z_snd.at[0], z_rcv.at[NZ], sibling)

    def factors_r():
        g = jnp.concatenate([pre_r[0, 0], pre_r[1, 0]], axis=0)
        u = jnp.concatenate([pre_r[0, 1], pre_r[1, 1]], axis=0)
        a, b = silu_factors(g, u)
        factor_r[0], factor_r[1] = a.T, b.T

    def factors_s():
        for half in range(2):
            a, b = silu_factors(pre_s[half, 0], pre_s[half, 1])
            factor_s[0, :, half * HID : (half + 1) * HID] = a
            factor_s[1, :, half * HID : (half + 1) * HID] = b

    def silu_grads(grad_hidden, factor):
        return (grad_hidden * factor[0]).astype(BF), (grad_hidden * factor[1]).astype(BF)

    def window(i):
        half, kind = divmod(i, 3)
        for c in range(CHIPS):
            q, o = divmod(c * CHUNK, LANES)
            wide = raw[i, :, q * LANES : (q + 2) * LANES] if o else None
            piece = raw[i, :, q * LANES : (q + 1) * LANES] if o == 0 else wide[:, o : o + LANES]
            col = (c % NX) * LANES
            win[kind, c // NX, half * HID : (half + 1) * HID, col : col + LANES] = piece

    def y_copy(rows, i):
        k = SLOTS[i]
        return remote(rows.at[x, 0], rows.at[x, i], gy_snd.at[k], gy_rcv.at[k], at_y(k)[1])

    def x_copy(rows, b, j, xx):
        part = rows.at[xx, pl.ds(*BATCHES[b])]
        i = b * NX + j
        return remote(part, part, gx_snd.at[i], gx_rcv.at[i], at_x(j)[1])

    def send_y(rows):
        for i in range(1, NY):
            y_copy(rows, i).start()

    def relay_x(rows):
        for b, (first, count) in enumerate(BATCHES):
            for i in range(first, first + count):
                if i:
                    y_copy(rows, i).wait_recv()
            for j in X_STEPS:
                x_copy(rows, b, j, x).start()

    def hidden(rows):
        acc = None
        for b, (first, count) in enumerate(BATCHES):
            for j in X_STEPS:
                x_copy(rows, b, j, lax.rem(x - j + NX, NX)).wait_recv()
            for i in range(first, first + count):
                yy = lax.rem(y - SLOTS[i] + NY, NY)
                wide = jnp.concatenate([rows[j, i] for j in range(NX)], axis=1)
                term = nt_dot(wide, win[0, yy])
                acc = term if acc is None else acc + term
        return acc

    def own_part(n, dg, du):
        for k in FAR_FIRST:
            yy = lax.rem(y + k, NY)
            t = nn_dot(dg, win[1, yy]) + nn_dot(du, win[2, yy])
            for j in range(NX):
                s = t[:, j * LANES : (j + 1) * LANES]
                four[j, 0:n] = s
                sums[yy, j, 0:n] = s.astype(BF)
            own[yy, 0:n] = four[x, 0:n]
            for j in X_STEPS:
                xx, dev = at_x(j)
                i = k * NX + j
                remote(
                    sums.at[yy, xx, pl.ds(0, n)], x_in.at[yy, j, pl.ds(0, n)],
                    rx_snd.at[i], rx_rcv.at[i], dev,
                ).start()

    def add_x(n, k):
        yy = lax.rem(y + k, NY)
        acc = own[yy, 0:n]
        for j in X_STEPS:
            i = k * NX + j
            remote(
                sums.at[yy, j, pl.ds(0, n)], x_in.at[yy, j, pl.ds(0, n)],
                rx_snd.at[i], rx_rcv.at[i], at_x(j)[1],
            ).wait_recv()
            acc += x_in[yy, j, 0:n].astype(F32)
        return acc

    def reduce(n):
        for k in FAR_FIRST[:-1]:
            y_out[k, 0:n] = add_x(n, k).astype(BF)
            remote(
                y_out.at[k, pl.ds(0, n)], y_in.at[k, pl.ds(0, n)], ry_snd.at[k], ry_rcv.at[k], at_y(k)[1]
            ).start()
        acc = add_x(n, 0)
        for k in NEAR_FIRST:
            remote(
                y_out.at[k, pl.ds(0, n)], y_in.at[k, pl.ds(0, n)], ry_snd.at[k], ry_rcv.at[k], at_y(k)[1]
            ).wait_recv()
            acc += y_in[k, 0:n].astype(F32)
        return acc

    def wait_sends(rows, n):
        for k in NEAR_FIRST:
            y_copy(rows, SLOTS.index(k)).wait_send()
            remote(
                y_out.at[k, pl.ds(0, n)], y_in.at[k, pl.ds(0, n)], ry_snd.at[k], ry_rcv.at[k], at_y(k)[1]
            ).wait_send()
        for k in range(NY):
            for j in X_STEPS:
                i = k * NX + j
                if k < len(BATCHES):
                    x_copy(rows, k, j, x).wait_send()
                remote(
                    sums.at[k, j, pl.ds(0, n)], x_in.at[k, j, pl.ds(0, n)],
                    rx_snd.at[i], rx_rcv.at[i], at_x(j)[1],
                ).wait_send()

    answer = remote(shared_sum.at[0], shared_sum.at[1], pair_snd.at[1], pair_rcv.at[1], sibling)
    pair_back = remote(z2_out.at[z], z2_in.at[z], z2_snd.at[NZ], z2_rcv.at[0], sibling)

    def wait_back(k, side):
        zz = lax.rem(z - k + NZ, NZ)
        i = side * NZ + k
        remote(z2_out.at[zz], z2_in.at[zz], z2_snd.at[i], z2_rcv.at[k], at_z(k, side)[1]).wait_recv()

    def token_rows():
        back = z2_in[...].reshape(NZ * 8, LANES)
        high = back.astype(BF)
        low = (back - high.astype(F32)).astype(BF)
        return nn_dot(place[...], high) + nn_dot(place[...], low)

    @pl.when(core == 0)
    def _():
        send_slots(0)
        pair.start()
        for c in swaps(shared_in, pre_s):
            c.start()
        z_in[0, z] = z_out[z]
        place[...] = placing.T.astype(BF)
        z2_out[...] = jnp.zeros_like(z2_out)
        loaded = local_loads(routed_in, pre_r)
        for i in range(5):
            loaded[i].wait()
        for i in range(3):
            window(i)
        pair_slots.wait_recv()
        for k in Z_STEPS[::-1]:
            wait_slots(0, k)
            wait_slots(1, k)
        for b in range(NZ):
            slots[b * CAP : (b + 1) * CAP] = z_in[0, b, 0:CAP] + z_in[1, b, 0:CAP]
        rows_r[x, 0] = slots[...].astype(BF)
        send_y(rows_r)
        arrive = swaps(routed_in, pre_r)
        arrive[3].wait_recv()
        arrive[4].wait_recv()
        factors_r()
        for i in range(3):
            arrive[i].wait_recv()
            window(3 + i)
        relay_x(rows_r)
        dg, du = silu_grads(hidden(rows_r), factor_r)
        own_part(ROUTED, dg, du)
        slots[...] = reduce(ROUTED)
        for b in range(NZ):
            z2_out[b, 0:CAP] = slots[b * CAP : (b + 1) * CAP]
        for k in Z_STEPS:
            for side in range(2):
                zz, dev = at_z(k, side)
                i = side * NZ + k
                remote(z2_out.at[zz], z2_in.at[z], z2_snd.at[i], z2_rcv.at[k], dev).start()
        pair_back.start()
        z2_in[z] = z2_out[z]
        wait_sends(rows_r, ROUTED)
        for c in swaps(shared_in, pre_s):
            c.wait_send()
        slots_sent()
        pair.wait_send()
        answer.wait_recv()
        for k in Z_STEPS[::-1]:
            wait_back(k, 0)
        out_ref[...] = (shared_sum[1] + token_rows()).T[0:FEAT].astype(BF)
        for k in range(1, NZ):
            for side in range(2):
                zz, dev = at_z(k, side)
                i = side * NZ + k
                remote(z2_out.at[zz], z2_in.at[z], z2_snd.at[i], z2_rcv.at[k], dev).wait_send()
        pair_back.wait_send()

    @pl.when(core == 1)
    def _():
        send_slots(1)
        pair_slots.start()
        pair.wait_recv()
        rows_s[x, 0] = placed[0] + placed[1]
        send_y(rows_s)
        for c in swaps(routed_in, pre_r):
            c.start()
        place[...] = placing.T.astype(BF)
        loaded = local_loads(shared_in, pre_s)
        for i in range(5):
            loaded[i].wait()
        for i in range(3):
            window(i)
        relay_x(rows_s)
        arrive = swaps(shared_in, pre_s)
        arrive[3].wait_recv()
        arrive[4].wait_recv()
        factors_s()
        for i in range(3):
            arrive[i].wait_recv()
            window(3 + i)
        dg, du = silu_grads(hidden(rows_s), factor_s)
        own_part(TOK, dg, du)
        shared_sum[0] = reduce(TOK)
        answer.start()
        wait_sends(rows_s, TOK)
        for c in swaps(routed_in, pre_r):
            c.wait_send()
        slots_sent()
        pair_slots.wait_send()
        answer.wait_send()
        pair_back.wait_recv()
        for k in Z_STEPS[::-1]:
            wait_back(k, 1)
        out_ref[...] = (shared_sum[0] + token_rows()).T[FEAT:CHUNK].astype(BF)


def body(
    grad_out, expert_index, slot_index, capacity, router_share,
    routed_gate, routed_up, gate_weight, up_weight, down_weight,
    shared_gate, shared_up, gate_common, up_common, down_common,
):
    dma = pltpu.SemaphoreType.DMA
    scratch = [
        pltpu.VMEM((FEAT, TOK), BF),
        pltpu.VMEM((1, TOK), jnp.int32), pltpu.VMEM((1, TOK), jnp.int32),
        pltpu.VMEM((1, NZ), jnp.int32), pltpu.VMEM((1, TOK), F32),
        pltpu.VMEM((2, 2, HID, ROUTED), BF), pltpu.VMEM((2, 2, TOK, HID), BF),
        pltpu.VMEM((2, ROUTED, 2 * HID), F32), pltpu.VMEM((2, TOK, 2 * HID), F32), pltpu.VMEM((2, TOK, LANES), BF),
        pltpu.VMEM((6, HID, WIDTH + LANES), BF),
        pltpu.VMEM((3, NY, 2 * HID, NX * LANES), BF),
        pltpu.VMEM((TOK, NZ * 8), BF),
        pltpu.VMEM((NZ, 8, LANES), F32), pltpu.VMEM((2, NZ, 8, LANES), F32),
        pltpu.VMEM((NZ, 8, LANES), F32), pltpu.VMEM((NZ, 8, LANES), F32),
        pltpu.VMEM((ROUTED, LANES), F32),
        pltpu.VMEM((NX, NY, ROUTED, LANES), BF), pltpu.VMEM((NX, NY, TOK, LANES), BF),
        pltpu.VMEM((NX, ROUTED, LANES), F32), pltpu.VMEM((NY, ROUTED, LANES), F32),
        pltpu.VMEM((NY, NX, ROUTED, LANES), BF), pltpu.VMEM((NY, NX, ROUTED, LANES), BF),
        pltpu.VMEM((NY, ROUTED, LANES), BF), pltpu.VMEM((NY, ROUTED, LANES), BF),
        pltpu.VMEM((2, TOK, LANES), F32),
        dma((10,)), dma((2,)), dma((2,)), dma((NZ,)), dma((2 * NZ,)), dma((2 * NZ,)), dma((NZ,)),
        dma((NY,)), dma((NY,)), dma((NY * NX,)), dma((NY * NX,)), dma((5,)), dma((5,)),
        dma((NY * NX,)), dma((NY * NX,)), dma((NY,)), dma((NY,)),
    ]
    out = pl.pallas_call(
        kernel,
        out_shape=jax.ShapeDtypeStruct((FEAT, TOK), BF),
        in_specs=[pl.BlockSpec(memory_space=pl.ANY)] * 15,
        out_specs=pl.BlockSpec(memory_space=pltpu.VMEM),
        scratch_shapes=scratch,
        compiler_params=pltpu.CompilerParams(
            collective_id=0, has_side_effects=True, vmem_limit_bytes=56 * 1024 * 1024
        ),
    )(
        grad_out.T, expert_index.reshape(1, -1), slot_index.reshape(1, -1), capacity.reshape(1, -1),
        router_share.reshape(1, -1), routed_gate.swapaxes(1, 2), routed_up.swapaxes(1, 2), gate_weight, up_weight, down_weight,
        shared_gate, shared_up, gate_common, up_common, down_common,
    )
    return out.T


def solution(mesh):
    return jax.shard_map(
        body,
        mesh=mesh,
        in_specs=(
            P("expert", "dp"), P("expert"), P("expert"), P(), P("expert"),
            P("expert", None, "dp"), P("expert", None, "dp"),
            P("expert", "dp", None), P("expert", "dp", None), P("expert", "dp", None),
            P("expert", "dp"), P("expert", "dp"),
            P("dp", None), P("dp", None), P("dp", None),
        ),
        out_specs=P("expert", "dp"),
        check_vma=False,
    )
```
